256 devices in a mesh: batch: 256 (over x, z, y, core).
Axes of the slice: x: 4, y: 4, z: 8, core: 2. Of those that a mesh axis runs over, the one named last changes fastest.
Arguments:
- pupil_vectors: bfloat16 [196608, 768], P('batch'), may hold values from -6 to 6
- caption_vectors: bfloat16 [196608, 768], P('batch'), may hold values from -6 to 6
- mentor_unscaled_entries: bfloat16 [196608, 768], P('batch'), may hold values from -6 to 6
- mentor_group_factors: float32 [196608, 24], P('batch'), may hold values from 0.25 to 2
- partner_replica_lag: int32 [196608], P('batch'), may hold values from 0 to 2
- partner_entry_slot: int32 [196608], P('batch'), may hold values from 0 to 767
- logit_multipliers: float32 [2], replicated, may hold values from 1 to 3
- logit_shifts: float32 [2], replicated, may hold values from -2 to 0
Outputs:
- row_loss: float32 [196608], P('batch')
- student_grad: bfloat16 [196608, 768], P('batch')
- text_grad: bfloat16 [196608, 768], P('batch')
The draws below stay inside these ranges and needn't reach their ends.
All inputs are finite; a program needn't handle non-finite values.
Results may differ from the reference program's by a relative error of at most 0.0039.
Values may be sent and summed in bfloat16 or wider, within the bound.
A program may use at most 64 MiB of HBM per device.

```python
import math
import jax
import jax.numpy as jnp
from jax import lax

FEATURE_SIZE = 768
QBLOCK = 32
TOK_DEV = 768
STEPS = 2
TOKENS = 196608
N_BATCH = 256


def with_ends(array, rng, least, largest):
    longest = array.shape.index(max(array.shape))
    spots = []
    for shift in (0, 1):
        where = [jax.random.randint(jax.random.fold_in(rng, axis), (), 0, length) for axis, length in enumerate(array.shape)]
        where[longest] = (where[longest] + shift) % array.shape[longest]
        spots.append(tuple(where))
    return array.at[spots[0]].set(least).at[spots[1]].set(largest)


def levels(key, shape, split, smallest, largest):
    factor_of, own = 1.0, jax.random.fold_in(key, 6)
    for axis_at, blocks in split:
        heights = jnp.exp(jax.random.uniform(jax.random.fold_in(own, axis_at), (blocks,), jnp.float32, smallest / len(split), largest / len(split)))
        factor_of = factor_of * jnp.repeat(heights, shape[axis_at] // blocks).reshape([-1 if axis == axis_at else 1 for axis in range(len(shape))])
    return factor_of


def gaussian(key, dims, scale, reach, cuts=(), kind=jnp.bfloat16):
    array = jax.random.normal(key, dims, jnp.float32) * scale
    if len(cuts) > 0:
        array = levels(key, dims, cuts, -0.22, 0.18) * array
    return jnp.clip(array, min=-reach, max=reach).astype(kind)


def setup_inputs(seed: int = 0) -> dict:
    keys = jax.random.split(jax.random.key(seed), 9)
    return {
        "pupil_vectors": gaussian(keys[0], (TOKENS, FEATURE_SIZE), 1.0, 6.0, ((0, 256),)),
        "caption_vectors": gaussian(keys[1], (TOKENS, FEATURE_SIZE), 1.0, 6.0, ((0, 256),)),
        "mentor_unscaled_entries": gaussian(keys[2], (TOKENS, FEATURE_SIZE), 1.0, 6.0, ((0, 256),)),
        "mentor_group_factors": jnp.clip(jnp.exp(math.log(2.0) - 2.0794415 * jax.random.uniform(keys[3], (TOKENS, FEATURE_SIZE // QBLOCK), jnp.float32) ** levels(keys[3], (TOKENS, FEATURE_SIZE // QBLOCK), ((0, 256),), -0.2, 0.2)), 0.25, 2.0),
        "partner_replica_lag": with_ends(jax.random.randint(keys[4], (TOKENS,), 0, STEPS + 1), jax.random.fold_in(keys[4], 1), 0, STEPS).astype(jnp.int32),
        "partner_entry_slot": with_ends(jax.random.randint(keys[5], (TOKENS,), 0, TOK_DEV), jax.random.fold_in(keys[5], 1), 0, TOK_DEV - 1).astype(jnp.int32),
        "logit_multipliers": jnp.clip(jnp.exp(jax.random.uniform(keys[6], (2,), jnp.float32, math.log(1.0), math.log(3.0))), 1.0, 3.0),
        "logit_shifts": jnp.clip(jax.random.uniform(keys[7], (2,), jnp.float32, -2.0, 0.0), -2.0, 0.0),
    }


def dequantize(values, scales):
    wide = jnp.repeat(scales, QBLOCK, axis=1)
    return (values.astype(jnp.float32) * wide).astype(jnp.bfloat16)

def caption_target_group(pupil_vector, caption_vector_list, iteration_total, location_slot, rotation_lag, logit_multipliers, logit_shifts):
    feature_size = pupil_vector.shape[1]
    objective_factor = logit_multipliers[0] / math.sqrt(feature_size)
    logit = objective_factor * jnp.dot(pupil_vector, caption_vector_list.T, preferred_element_type=jnp.float32) + logit_shifts[0]
    columns = jnp.arange(caption_vector_list.shape[0], dtype=jnp.int32)
    hit = (iteration_total[:, None] == rotation_lag) & (location_slot[:, None] == columns[None, :])
    sign = jnp.where(hit, jnp.float32(1.0), jnp.float32(-1.0))
    terms = lax.optimization_barrier(jnp.sum(jax.nn.softplus(-sign * logit), axis=1))
    slope = (-sign * jax.nn.sigmoid(-sign * logit)).astype(jnp.bfloat16)
    return (terms, slope)

def mentor_target_group(pupil_vector, mentor_vector, rotation_lag, logit_multipliers, logit_shifts):
    feature_size = pupil_vector.shape[1]
    objective_factor = logit_multipliers[1] / math.sqrt(feature_size)
    logit = objective_factor * jnp.dot(pupil_vector, mentor_vector.T, preferred_element_type=jnp.float32) + logit_shifts[1]
    rows_here = jnp.arange(pupil_vector.shape[0], dtype=jnp.int32)
    hit = (rows_here[:, None] == rows_here[None, :]) & (rotation_lag == 0)
    sign = jnp.where(hit, jnp.float32(1.0), jnp.float32(-1.0))
    terms = lax.optimization_barrier(jnp.sum(jax.nn.softplus(-sign * logit), axis=1))
    slope = (-sign * jax.nn.sigmoid(-sign * logit)).astype(jnp.bfloat16)
    return (terms, slope)

def reference(pupil_vectors, caption_vectors, mentor_unscaled_entries, mentor_group_factors, partner_replica_lag, partner_entry_slot, logit_multipliers, logit_shifts):
    teacher = dequantize(mentor_unscaled_entries, mentor_group_factors)
    count = N_BATCH
    pupil_vector_list = pupil_vectors.reshape(count, TOK_DEV, FEATURE_SIZE)
    caption_vector_list = caption_vectors.reshape(count, TOK_DEV, FEATURE_SIZE)
    mentor_vector = teacher.reshape(count, TOK_DEV, FEATURE_SIZE)
    iteration_total = partner_replica_lag.reshape(count, TOK_DEV)
    location_slot = partner_entry_slot.reshape(count, TOK_DEV)
    caption_factor = logit_multipliers[0] / math.sqrt(FEATURE_SIZE)
    mentor_factor = logit_multipliers[1] / math.sqrt(FEATURE_SIZE)

    def per_device(replica_label):
        pupil_vector = pupil_vector_list[replica_label]
        total = jnp.zeros((TOK_DEV,), jnp.float32)
        grad = jnp.zeros((TOK_DEV, FEATURE_SIZE), jnp.float32)
        for rotation_lag in range(STEPS + 1):
            holder_replica = ((replica_label - rotation_lag) % count).astype(jnp.int32)
            caption_penalty_parts, caption_gradient_share = caption_target_group(pupil_vector, caption_vector_list[holder_replica], iteration_total[replica_label], location_slot[replica_label], rotation_lag, logit_multipliers, logit_shifts)
            mentor_penalty_parts, mentor_gradient_share = mentor_target_group(pupil_vector, mentor_vector[holder_replica], rotation_lag, logit_multipliers, logit_shifts)
            total = total + caption_penalty_parts + mentor_penalty_parts
            grad = grad + caption_factor * jnp.dot(caption_gradient_share, caption_vector_list[holder_replica], preferred_element_type=jnp.float32)
            grad = grad + mentor_factor * jnp.dot(mentor_gradient_share, mentor_vector[holder_replica], preferred_element_type=jnp.float32)
        return (total / ((STEPS + 1) * TOK_DEV), grad.astype(jnp.bfloat16))

    def per_owner(holder_replica):
        acc = jnp.zeros((TOK_DEV, FEATURE_SIZE), jnp.float32)
        for rotation_lag in range(STEPS + 1):
            replica_label = ((holder_replica + rotation_lag) % count).astype(jnp.int32)
            discarded_output, caption_gradient_share = caption_target_group(pupil_vector_list[replica_label], caption_vector_list[holder_replica], iteration_total[replica_label], location_slot[replica_label], rotation_lag, logit_multipliers, logit_shifts)
            acc = acc + caption_factor * jnp.dot(caption_gradient_share.T, pupil_vector_list[replica_label], preferred_element_type=jnp.float32)
        return acc.astype(jnp.bfloat16)
    devices = jnp.arange(count, dtype=jnp.int32)
    losses, grads = lax.map(per_device, devices)
    text_grads = lax.map(per_owner, devices)
    return (losses.reshape(TOKENS), grads.reshape(TOKENS, FEATURE_SIZE), text_grads.reshape(TOKENS, FEATURE_SIZE))
```

```python
import math

import jax
import jax.numpy as jnp
from jax import lax
from jax.experimental import pallas as pl
from jax.experimental.pallas import tpu as pltpu
from jax.sharding import PartitionSpec as P

F32 = jnp.float32
BF16 = jnp.bfloat16
MESH = pl.DeviceIdType.MESH
LN2 = math.log(2.0)
TILE = 256


def dot(a, b, ca, cb):
    return lax.dot_general(a, b, (((ca,), (cb,)), ((), ())), preferred_element_type=F32)


def score(students, refs, factors, shifts, hits, slopes):
    count = students.shape[0]
    width = refs[0].shape[0]
    total = jnp.zeros((1, count), F32)
    for ref, factor, shift, hit_row, slope in zip(refs, factors, shifts, hits, slopes):
        product = jnp.ones((8, count), F32)
        excess = jnp.zeros((8, count), F32)
        for start in range(0, width, TILE):
            half = dot(ref[start:start + TILE, :], students, 1, 1) * factor + shift
            sign = None
            if hit_row is not None:
                rows = lax.broadcasted_iota(jnp.int32, (TILE, count), 0)
                sign = jnp.where(rows == hit_row - start, F32(-1.0), F32(1.0))
                half = half * sign
            tanh = jnp.tanh(half)
            doubled = 1.0 + tanh
            if sign is not None:
                doubled = doubled * sign
            slope[start:start + TILE, :] = doubled.astype(BF16)
            folded = (1.0 + jnp.abs(tanh)).reshape(TILE // 8, 8, count)
            positive = jnp.maximum(half, 0.0).reshape(TILE // 8, 8, count)
            for part in range(TILE // 8):
                product = product * folded[part]
                excess = excess + positive[part]
        terms = 2.0 * excess - jnp.log(product)
        total = total + (jnp.sum(terms, axis=0, keepdims=True) + F32(width * LN2))
    return total


def kernel(
    steps,
    x_hbm, t_hbm, m_hbm, scales, lag, slot, multipliers, shifts,
    loss_out, sg_hbm, tg_hbm,
    xb, text, teacher, raw, slope_t, slope_m, slope_t2, slope_m2,
    tg_own, tg_other, g_step, g_local, g_send, g_back, tg_send, tg_back, sg_stage, tg_stage,
    code_mine, code_far, loss_mine, loss_far, loss_back,
    x_ss, x_rs, g_ss, g_rs, pair_ss, pair_rs, small_ss, small_rs, load, store,
):
    rows, width = tg_own.shape
    chunk = rows // steps
    devices = lax.axis_size("batch")
    me = lax.axis_index("batch")
    core = lax.rem(me, 2)
    other = me + 1 - 2 * core
    behind = lax.rem(me + devices - 2, devices)
    ahead = lax.rem(me + 2, devices)

    barrier = pltpu.get_barrier_semaphore()
    for partner in (other, behind, ahead):
        pl.semaphore_signal(barrier, inc=1, device_id=(partner,), device_id_type=MESH)

    load_m = pltpu.make_async_copy(m_hbm, raw, load.at[0])
    load_m.start()
    load_t = pltpu.make_async_copy(t_hbm, text.at[0], load.at[1])
    load_t.start()
    load_x = [
        pltpu.make_async_copy(
            x_hbm.at[pl.ds(i * chunk, chunk)], xb.at[i, pl.ds(chunk, chunk)], load.at[2 + i]
        )
        for i in range(steps)
    ]
    for copy in load_x:
        copy.start()

    code_mine[...] = lag[...] * rows + slot[...]
    pl.semaphore_wait(barrier, 3)

    def remote(src, dst, send, recv, device):
        return pltpu.make_async_remote_copy(
            src_ref=src, dst_ref=dst, send_sem=send, recv_sem=recv,
            device_id=(device,), device_id_type=MESH,
        )

    def x_copy(i):
        return remote(
            x_hbm.at[pl.ds(i * chunk, chunk)], xb.at[i, pl.ds(0, chunk)], x_ss.at[i], x_rs.at[i], behind
        )

    def g_copy(i):
        return remote(g_send.at[i], g_back.at[i], g_ss.at[i], g_rs.at[i], ahead)

    code_copy = remote(code_mine, code_far, small_ss.at[0], small_rs.at[0], behind)
    loss_copy = remote(loss_far, loss_back, small_ss.at[1], small_rs.at[1], ahead)
    text_copy = remote(t_hbm, text.at[1], pair_ss.at[0], pair_rs.at[0], other)
    teacher_copy = remote(teacher.at[0], teacher.at[1], pair_ss.at[1], pair_rs.at[1], other)
    tg_copy = remote(tg_send, tg_back, pair_ss.at[2], pair_rs.at[2], other)

    code_copy.start()
    for i in range(steps):
        x_copy(i).start()
    text_copy.start()

    groups = scales.shape[0]
    exact = scales[...]
    high = exact.astype(BF16).astype(F32)
    middle = (exact - high).astype(BF16).astype(F32)
    low = exact - high - middle
    pieces = jnp.concatenate([high, middle, low], axis=0).astype(BF16)
    spread_rows = lax.rem(lax.broadcasted_iota(jnp.int32, (3 * groups, width), 0), groups)
    spread_cols = lax.broadcasted_iota(jnp.int32, (3 * groups, width), 1) // (width // groups)
    spread = jnp.where(spread_rows == spread_cols, F32(1.0), F32(0.0)).astype(BF16)
    load_m.wait()
    for start in range(0, rows, TILE):
        wide = dot(pieces[:, start:start + TILE], spread, 0, 0)
        teacher[0, start:start + TILE, :] = (raw[start:start + TILE, :].astype(F32) * wide).astype(BF16)
    teacher_copy.start()

    scale = F32(0.5 / math.sqrt(width))
    factor_t = multipliers[0] * scale
    factor_m = multipliers[1] * scale
    shift_t = shifts[0] * 0.5
    shift_m = shifts[1] * 0.5

    tg_own[...] = jnp.zeros_like(tg_own)
    tg_other[...] = jnp.zeros_like(tg_other)
    load_t.wait()
    for copy in load_x:
        copy.wait()
    code_copy.wait()
    text_copy.wait()
    teacher_copy.wait()

    lanes = lax.broadcasted_iota(jnp.int32, (1, chunk), 1)
    nowhere = jnp.full((1, chunk), -1, jnp.int32)

    def at_lag(code, k):
        return code - k * rows

    def step(i, carry):
        x_copy(i).wait_recv()
        far = code_far[pl.ds(i, 1), :]
        near = code_mine[pl.ds(i, 1), :]
        hit_t = jnp.concatenate([at_lag(far, 2), at_lag(near, 0)], axis=1)
        hit_m = jnp.concatenate([nowhere, lanes + i * chunk], axis=1)
        both = xb[i]
        loss = score(
            both, (text.at[0], teacher.at[0]), (factor_t, factor_m), (shift_t, shift_m),
            (hit_t, hit_m), (slope_t, slope_m),
        )
        loss_far[pl.ds(i, 1), :] = loss[:, :chunk]
        loss_mine[pl.ds(i, 1), :] = loss[:, chunk:]

        place = pl.multiple_of(core * chunk, chunk)
        picked = xb[i, pl.ds(place, chunk), :]
        on_far = (core == 0)
        code = jnp.where(on_far, far, near)
        loss2 = score(
            picked, (text.at[1], teacher.at[1]), (factor_t, factor_m), (shift_t, shift_m),
            (at_lag(code, 1), None), (slope_t2, slope_m2),
        )
        loss_far[pl.ds(i, 1), :] += jnp.where(on_far, loss2, 0.0)
        loss_mine[pl.ds(i, 1), :] += jnp.where(on_far, 0.0, loss2)

        g_step[...] = (
            dot(slope_t[...], text[0], 0, 0) * factor_t + dot(slope_m[...], teacher[0], 0, 0) * factor_m
        )
        g_step[pl.ds(place, chunk), :] += (
            dot(slope_t2[...], text[1], 0, 0) * factor_t + dot(slope_m2[...], teacher[1], 0, 0) * factor_m
        )
        g_send[i] = g_step[:chunk, :].astype(BF16)
        g_copy(i).start()
        g_local[pl.ds(i * chunk, chunk), :] = g_step[chunk:, :]
        tg_own[...] += dot(slope_t[...], both, 1, 0)
        tg_other[...] += dot(slope_t2[...], picked, 1, 0)
        return carry

    lax.fori_loop(0, steps, step, 0)

    loss_copy.start()
    tg_send[...] = tg_other[...].astype(BF16)
    tg_copy.start()

    for i in range(steps):
        at = pl.ds(i * chunk, chunk)
        g_copy(i).wait_recv()
        sg_stage[at, :] = (g_local[at, :] + g_back[i].astype(F32)).astype(BF16)
        pltpu.make_async_copy(sg_stage.at[at], sg_hbm.at[at], store.at[i]).start()
        if i == 0:
            tg_copy.wait()
            tg_stage[...] = ((tg_own[...] + tg_back[...].astype(F32)) * factor_t).astype(BF16)
            store_tg = pltpu.make_async_copy(tg_stage, tg_hbm, store.at[steps])
            store_tg.start()
    loss_copy.wait()
    loss_out[...] = (loss_mine[...] + loss_back[...]) * F32(1.0 / (3 * rows))

    for i in range(steps):
        at = pl.ds(i * chunk, chunk)
        x_copy(i).wait_send()
        g_copy(i).wait_send()
        pltpu.make_async_copy(sg_stage.at[at], sg_hbm.at[at], store.at[i]).wait()
    store_tg.wait()


def body(
    pupil_vectors,
    caption_vectors,
    mentor_unscaled_entries,
    mentor_group_factors,
    partner_replica_lag,
    partner_entry_slot,
    logit_multipliers,
    logit_shifts,
):
    rows, width = pupil_vectors.shape
    steps = 6
    chunk = rows // steps
    hbm = pl.BlockSpec(memory_space=pl.ANY)
    vmem = pl.BlockSpec(memory_space=pltpu.VMEM)
    smem = pl.BlockSpec(memory_space=pltpu.SMEM)
    full_bf16 = pltpu.VMEM((rows, width), BF16)
    full_f32 = pltpu.VMEM((rows, width), F32)
    small_f32 = pltpu.VMEM((steps, chunk), F32)
    small_i32 = pltpu.VMEM((steps, chunk), jnp.int32)
    dma = pltpu.SemaphoreType.DMA
    loss, student_grad, text_grad = pl.pallas_call(
        lambda *refs: kernel(steps, *refs),
        name="distill",
        out_shape=(
            jax.ShapeDtypeStruct((steps, chunk), F32),
            jax.ShapeDtypeStruct((rows, width), BF16),
            jax.ShapeDtypeStruct((rows, width), BF16),
        ),
        in_specs=[hbm, hbm, hbm, vmem, vmem, vmem, smem, smem],
        out_specs=(vmem, hbm, hbm),
        scratch_shapes=[
            pltpu.VMEM((steps, 2 * chunk, width), BF16),
            pltpu.VMEM((2, rows, width), BF16),
            pltpu.VMEM((2, rows, width), BF16),
            full_bf16,
            pltpu.VMEM((rows, 2 * chunk), BF16),
            pltpu.VMEM((rows, 2 * chunk), BF16),
            pltpu.VMEM((rows, chunk), BF16),
            pltpu.VMEM((rows, chunk), BF16),
            full_f32,
            full_f32,
            pltpu.VMEM((2 * chunk, width), F32),
            full_f32,
            pltpu.VMEM((steps, chunk, width), BF16),
            pltpu.VMEM((steps, chunk, width), BF16),
            full_bf16,
            full_bf16,
            full_bf16,
            full_bf16,
            small_i32, small_i32, small_f32, small_f32, small_f32,
            dma((steps,)), dma((steps,)), dma((steps,)), dma((steps,)),
            dma((3,)), dma((3,)), dma((2,)), dma((2,)),
            dma((2 + steps,)), dma((steps + 1,)),
        ],
        compiler_params=pltpu.CompilerParams(
            collective_id=0, has_side_effects=True, vmem_limit_bytes=56 * 1024 * 1024
        ),
        cost_estimate=pl.CostEstimate(
            flops=30 * rows * rows * width, bytes_accessed=12 * rows * width, transcendentals=6 * rows * rows
        ),
    )(
        pupil_vectors,
        caption_vectors,
        mentor_unscaled_entries,
        mentor_group_factors.T,
        partner_replica_lag.reshape(steps, chunk),
        partner_entry_slot.reshape(steps, chunk),
        logit_multipliers,
        logit_shifts,
    )
    return loss.reshape(rows), student_grad, text_grad


def solution(mesh):
    placed = (
        P("batch", None),
        P("batch", None),
        P("batch", None),
        P("batch", None),
        P("batch"),
        P("batch"),
        P(),
        P(),
    )
    return jax.shard_map(
        body,
        mesh=mesh,
        in_specs=placed,
        out_specs=(P("batch"), P("batch", None), P("batch", None)),
        check_vma=False,
    )
```

```python
import math

import jax
import jax.numpy as jnp
from jax import lax
from jax.experimental import pallas as pl
from jax.experimental.pallas import tpu as pltpu
from jax.sharding import PartitionSpec as P

F32 = jnp.float32
BF16 = jnp.bfloat16
MESH = pl.DeviceIdType.MESH
LN2 = math.log(2.0)
TILE = 256
CHUNK = 128


def dot(a, b, ca, cb):
    return lax.dot_general(a, b, (((ca,), (cb,)), ((), ())), preferred_element_type=F32)


def score(students, refs, factors, shifts, hits, slopes):
    count = students.shape[0]
    width = refs[0].shape[0]
    total = jnp.zeros((1, count), F32)
    for ref, factor, shift, hit_row, slope in zip(refs, factors, shifts, hits, slopes):
        product = jnp.ones((8, count), F32)
        excess = jnp.zeros((8, count), F32)
        for start in range(0, width, TILE):
            half = dot(ref[start:start + TILE, :], students, 1, 1) * factor + shift
            sign = None
            if hit_row is not None:
                rows = lax.broadcasted_iota(jnp.int32, (TILE, count), 0)
                sign = jnp.where(rows == hit_row - start, F32(-1.0), F32(1.0))
                half = half * sign
            tanh = jnp.tanh(half)
            doubled = 1.0 + tanh
            if sign is not None:
                doubled = doubled * sign
            slope[start:start + TILE, :] = doubled.astype(BF16)
            folded = (1.0 + jnp.abs(tanh)).reshape(TILE // 8, 8, count)
            positive = jnp.maximum(half, 0.0).reshape(TILE // 8, 8, count)
            for part in range(TILE // 8):
                product = product * folded[part]
                excess = excess + positive[part]
        terms = 2.0 * excess - jnp.log(product)
        total = total + (jnp.sum(terms, axis=0, keepdims=True) + F32(width * LN2))
    return total


def kernel(
    chunk,
    x_hbm, t_hbm, m_hbm, scales_hbm, lag_hbm, slot_hbm, multipliers_hbm, shifts_hbm,
    loss_out, sg_out, tg_out,
    scales, lag, slot, multipliers, shifts,
    near, far, text, teacher, raw, near_t, near_m, far_t, part_t, far_m,
    tg_own, tg_other, g_step, g_local, g_send, g_back, tg_send, tg_back,
    code_mine, code_far, loss_mine, loss_far, loss_back,
    x_ss, x_rs, g_ss, g_rs, pair_ss, pair_rs, small_ss, small_rs, load,
):
    rows, width = tg_own.shape
    lanes = lag.shape[1]
    steps = rows // chunk
    wide_steps = rows // TILE
    devices = lax.axis_size("batch")
    me = lax.axis_index("batch")
    core = lax.rem(me, 2)
    other = me + 1 - 2 * core
    behind = lax.rem(me + devices - 2, devices)
    ahead = lax.rem(me + 2, devices)

    barrier = pltpu.get_barrier_semaphore()
    for partner in (other, behind, ahead):
        pl.semaphore_signal(barrier, inc=1, device_id=(partner,), device_id_type=MESH)

    load_m = pltpu.make_async_copy(m_hbm, raw, load.at[0])
    load_t = pltpu.make_async_copy(t_hbm, text.at[0], load.at[1])
    load_x = pltpu.make_async_copy(x_hbm, near, load.at[2])
    small = [
        pltpu.make_async_copy(source, held, load.at[3 + i])
        for i, (source, held) in enumerate((
            (lag_hbm, lag), (slot_hbm, slot), (scales_hbm, scales),
            (multipliers_hbm, multipliers), (shifts_hbm, shifts),
        ))
    ]
    for copy in small:
        copy.start()
    load_m.start()
    load_t.start()
    load_x.start()
    small[0].wait()
    small[1].wait()
    code_mine[...] = lag[...] * rows + slot[...]
    pl.semaphore_wait(barrier, 3)

    def remote(src, dst, send, recv, device):
        return pltpu.make_async_remote_copy(
            src_ref=src, dst_ref=dst, send_sem=send, recv_sem=recv,
            device_id=(device,), device_id_type=MESH,
        )

    def x_copy(i):
        at = pl.ds(i * chunk, chunk)
        return remote(x_hbm.at[at], far.at[at], x_ss.at[i], x_rs.at[i], behind)

    def g_copy(i):
        at = pl.ds(i * chunk, chunk)
        return remote(g_send.at[at], g_back.at[at], g_ss.at[i], g_rs.at[i], ahead)

    code_copy = remote(code_mine, code_far, small_ss.at[0], small_rs.at[0], behind)
    loss_copy = remote(loss_far, loss_back, small_ss.at[1], small_rs.at[1], ahead)
    text_copy = remote(t_hbm, text.at[1], pair_ss.at[0], pair_rs.at[0], other)
    teacher_copy = remote(teacher.at[0], teacher.at[1], pair_ss.at[1], pair_rs.at[1], other)
    tg_copy = remote(tg_send, tg_back, pair_ss.at[2], pair_rs.at[2], other)

    code_copy.start()
    for i in range(steps):
        x_copy(i).start()
    text_copy.start()

    for copy in small[2:]:
        copy.wait()
    groups = scales.shape[0]
    exact = scales[...]
    high = exact.astype(BF16).astype(F32)
    middle = (exact - high).astype(BF16).astype(F32)
    low = exact - high - middle
    pieces = jnp.concatenate([high, middle, low], axis=0).astype(BF16)
    spread_rows = lax.rem(lax.broadcasted_iota(jnp.int32, (3 * groups, width), 0), groups)
    spread_cols = lax.broadcasted_iota(jnp.int32, (3 * groups, width), 1) // (width // groups)
    spread = jnp.where(spread_rows == spread_cols, F32(1.0), F32(0.0)).astype(BF16)
    load_m.wait()
    for start in range(0, rows, TILE):
        wide = dot(pieces[:, start:start + TILE], spread, 0, 0)
        teacher[0, start:start + TILE, :] = (raw[start:start + TILE, :].astype(F32) * wide).astype(BF16)
    teacher_copy.start()

    scale = F32(0.5 / math.sqrt(width))
    factors = (multipliers[0] * scale, multipliers[1] * scale)
    halves = (shifts[0] * 0.5, shifts[1] * 0.5)

    def students_grad(slope_t, slope_m, k):
        return dot(slope_t[...], text[k], 0, 0) * factors[0] + dot(slope_m[...], teacher[k], 0, 0) * factors[1]

    def near_step(k, n, carry):
        at = pl.ds(pl.multiple_of(n * TILE, TILE), TILE)
        per = TILE // lanes
        code = jnp.concatenate([code_mine[pl.ds(n * per + p, 1), :] for p in range(per)], axis=1)
        diagonal = lax.broadcasted_iota(jnp.int32, (1, TILE), 1) + n * TILE if k == 0 else None
        slope_t, slope_m = near_t.at[k, :, at], near_m
        loss = score(
            near[at, :], (text.at[k], teacher.at[k]), factors, halves, (code - k * rows, diagonal),
            (slope_t, slope_m),
        )
        grad = students_grad(slope_t, slope_m, k)
        for p in range(per):
            row = pl.ds(n * per + p, 1)
            part = loss[:, p * lanes:(p + 1) * lanes]
            loss_mine[row, :] = part if k == 0 else loss_mine[row, :] + part
        g_local[at, :] = grad if k == 0 else g_local[at, :] + grad
        return carry

    load_t.wait()
    load_x.wait()
    lax.fori_loop(0, wide_steps, lambda n, carry: near_step(0, n, carry), 0)
    code_copy.wait()
    text_copy.wait()
    teacher_copy.wait()

    per = lanes // chunk

    def far_job(k, i, part, code):
        at = pl.ds(pl.multiple_of(i * chunk, chunk), chunk)
        slope_t, slope_m = part_t.at[part, k], far_m
        loss = score(
            far[at, :], (text.at[k], teacher.at[k]), factors, halves, (code - (2 - k) * rows, None),
            (slope_t, slope_m),
        )
        grad = students_grad(slope_t, slope_m, k)
        place = (pl.ds(i // per, 1), pl.ds(part * chunk, chunk))
        loss_far[place] = loss if k == 0 else loss_far[place] + loss
        g_step[...] = grad if k == 0 else g_step[...] + grad

    def keep_slopes(k, outer):
        columns = pl.ds(pl.multiple_of(outer * lanes, lanes), lanes)
        far_t[k, :, columns] = jnp.concatenate([part_t[part, k] for part in range(per)], axis=1)

    def far_step(outer, carry):
        for part in range(per):
            i = outer * per + part
            x_copy(i).wait_recv()
            code = code_far[pl.ds(outer, 1), pl.ds(part * chunk, chunk)]
            far_job(0, i, part, code)

            @pl.when(core == 0)
            def _():
                far_job(1, i, part, code)

            g_send[pl.ds(pl.multiple_of(i * chunk, chunk), chunk), :] = g_step[...].astype(BF16)
            g_copy(i).start()
        keep_slopes(0, outer)

        @pl.when(core == 0)
        def _():
            keep_slopes(1, outer)

        @pl.when(jnp.logical_and(core == 1, lax.rem(outer, 2) == 0))
        def _():
            near_step(1, outer // 2, 0)
        return carry

    lax.fori_loop(0, rows // lanes, far_step, 0)
    loss_copy.start()

    @pl.when(core == 0)
    def _():
        tg_other[...] = dot(far_t[1], far[...], 1, 0)

    @pl.when(core == 1)
    def _():
        tg_other[...] = dot(near_t[1], near[...], 1, 0)

    tg_send[...] = tg_other[...].astype(BF16)
    tg_copy.start()
    tg_own[...] = dot(near_t[0], near[...], 1, 0)
    tg_own[...] += dot(far_t[0], far[...], 1, 0)

    for i in range(steps):
        at = pl.ds(i * chunk, chunk)
        g_copy(i).wait_recv()
        sg_out[at, :] = (g_local[at, :] + g_back[at, :].astype(F32)).astype(BF16)
        if i == steps // 2:
            tg_copy.wait()
            tg_out[...] = ((tg_own[...] + tg_back[...].astype(F32)) * factors[0]).astype(BF16)
    loss_copy.wait()
    loss_out[...] = (loss_mine[...] + loss_back[...]) * F32(1.0 / (3 * rows))
    for i in range(steps):
        x_copy(i).wait_send()
        g_copy(i).wait_send()


def write_out(*refs):
    count = len(refs) // 2
    done = refs[-1]
    copies = [pltpu.make_async_copy(refs[i], refs[count + i], done.at[i]) for i in range(count)]
    for copy in copies:
        copy.start()
    for copy in copies:
        copy.wait()


def body(
    pupil_vectors,
    caption_vectors,
    mentor_unscaled_entries,
    mentor_group_factors,
    partner_replica_lag,
    partner_entry_slot,
    logit_multipliers,
    logit_shifts,
):
    rows, width = pupil_vectors.shape
    chunk = CHUNK
    steps = rows // chunk
    lanes = 128
    hbm = pl.BlockSpec(memory_space=pl.ANY)
    vmem = pl.BlockSpec(memory_space=pltpu.VMEM)
    full_bf16 = pltpu.VMEM((rows, width), BF16)
    full_f32 = pltpu.VMEM((rows, width), F32)
    small_f32 = pltpu.VMEM((rows // lanes, lanes), F32)
    small_i32 = pltpu.VMEM((rows // lanes, lanes), jnp.int32)
    dma = pltpu.SemaphoreType.DMA
    results = pl.pallas_call(
        lambda *refs: kernel(chunk, *refs),
        name="distill",
        out_shape=(
            pltpu.VMEM((rows // lanes, lanes), F32),
            pltpu.VMEM((rows, width), BF16),
            pltpu.VMEM((rows, width), BF16),
        ),
        in_specs=[hbm] * 8,
        out_specs=(vmem, vmem, vmem),
        scratch_shapes=[
            pltpu.VMEM(mentor_group_factors.shape[::-1], F32),
            small_i32,
            small_i32,
            pltpu.SMEM(logit_multipliers.shape, F32),
            pltpu.SMEM(logit_shifts.shape, F32),
            full_bf16,
            full_bf16,
            pltpu.VMEM((2, rows, width), BF16),
            pltpu.VMEM((2, rows, width), BF16),
            full_bf16,
            pltpu.VMEM((2, rows, rows), BF16),
            pltpu.VMEM((rows, TILE), BF16),
            pltpu.VMEM((2, rows, rows), BF16),
            pltpu.VMEM((lanes // chunk, 2, rows, chunk), BF16),
            pltpu.VMEM((rows, chunk), BF16),
            full_f32,
            full_f32,
            pltpu.VMEM((chunk, width), F32),
            full_f32,
            full_bf16,
            full_bf16,
            full_bf16,
            full_bf16,
            small_i32, small_i32, small_f32, small_f32, small_f32,
            dma((steps,)), dma((steps,)), dma((steps,)), dma((steps,)),
            dma((3,)), dma((3,)), dma((2,)), dma((2,)),
            dma((8,)),
        ],
        compiler_params=pltpu.CompilerParams(
            collective_id=0, has_side_effects=True, vmem_limit_bytes=56 * 1024 * 1024
        ),
        cost_estimate=pl.CostEstimate(
            flops=30 * rows * rows * width, bytes_accessed=12 * rows * width, transcendentals=6 * rows * rows
        ),
    )(
        pupil_vectors,
        caption_vectors,
        mentor_unscaled_entries,
        mentor_group_factors.T,
        partner_replica_lag.reshape(rows // lanes, lanes),
        partner_entry_slot.reshape(rows // lanes, lanes),
        logit_multipliers,
        logit_shifts,
    )
    loss, student_grad, text_grad = pl.pallas_call(
        write_out,
        name="write_out",
        out_shape=(
            jax.ShapeDtypeStruct((rows // lanes, lanes), F32),
            jax.ShapeDtypeStruct((rows, width), BF16),
            jax.ShapeDtypeStruct((rows, width), BF16),
        ),
        in_specs=[vmem, vmem, vmem],
        out_specs=(hbm, hbm, hbm),
        scratch_shapes=[dma((3,))],
    )(*(pltpu.with_memory_space_constraint(result, pltpu.VMEM) for result in results))
    return loss.reshape(rows), student_grad, text_grad


def solution(mesh):
    placed = (
        P("batch", None),
        P("batch", None),
        P("batch", None),
        P("batch", None),
        P("batch"),
        P("batch"),
        P(),
        P(),
    )
    return jax.shard_map(
        body,
        mesh=mesh,
        in_specs=placed,
        out_specs=(P("batch"), P("batch", None), P("batch", None)),
        check_vma=False,
    )
```

```python
import math

import jax
import jax.numpy as jnp
from jax import lax
from jax.experimental import pallas as pl
from jax.experimental.pallas import tpu as pltpu
from jax.sharding import PartitionSpec as P

F32 = jnp.float32
BF16 = jnp.bfloat16
MESH = pl.DeviceIdType.MESH
LN2 = math.log(2.0)
TILE = 256
CHUNK = 96


def dot(a, b, ca, cb):
    return lax.dot_general(a, b, (((ca,), (cb,)), ((), ())), preferred_element_type=F32)


def score(students, refs, factors, shifts, hits, slopes):
    count = students.shape[0]
    width = refs[0].shape[0]
    total = jnp.zeros((1, count), F32)
    for ref, factor, shift, hit_row, slope in zip(refs, factors, shifts, hits, slopes):
        product = jnp.ones((8, count), F32)
        excess = jnp.zeros((8, count), F32)
        for start in range(0, width, TILE):
            half = dot(ref[start:start + TILE, :], students, 1, 1) * factor + shift
            sign = None
            if hit_row is not None:
                rows = lax.broadcasted_iota(jnp.int32, (TILE, count), 0)
                sign = jnp.where(rows == hit_row - start, F32(-1.0), F32(1.0))
                half = half * sign
            tanh = jnp.tanh(half)
            doubled = 1.0 + tanh
            if sign is not None:
                doubled = doubled * sign
            slope[start:start + TILE, :] = doubled.astype(BF16)
            folded = (1.0 + jnp.abs(tanh)).reshape(TILE // 8, 8, count)
            positive = jnp.maximum(half, 0.0).reshape(TILE // 8, 8, count)
            for part in range(TILE // 8):
                product = product * folded[part]
                excess = excess + positive[part]
        terms = 2.0 * excess - jnp.log(product)
        total = total + (jnp.sum(terms, axis=0, keepdims=True) + F32(width * LN2))
    return total


def regroup(source, target):
    long, short = source.shape[1], target.shape[1]
    for row in range(target.shape[0]):
        done = 0
        while done < short:
            line, column = divmod(row * short + done, long)
            count = min(short - done, long - column)
            target[row:row + 1, done:done + count] = source[line:line + 1, column:column + count]
            done += count


def kernel(
    chunk,
    x_hbm, t_hbm, m_hbm, scales_hbm, lag_hbm, slot_hbm, multipliers_hbm, shifts_hbm,
    loss_out, sg_out, tg_out,
    scales, lag, slot, multipliers, shifts,
    near, far, text, teacher, raw, near_t, near_m, far_t, far_m,
    tg_own, tg_other, g_local, g_send, g_back, tg_send, tg_back,
    code_mine, code_send, code_far, loss_mine, loss_far, loss_back, loss_wide,
    x_ss, x_rs, g_ss, g_rs, pair_ss, pair_rs, small_ss, small_rs, load,
):
    rows, width = tg_own.shape
    lanes = lag.shape[1]
    steps = rows // chunk
    wide_steps = rows // TILE
    devices = lax.axis_size("batch")
    me = lax.axis_index("batch")
    core = lax.rem(me, 2)
    other = me + 1 - 2 * core
    behind = lax.rem(me + devices - 2, devices)
    ahead = lax.rem(me + 2, devices)

    barrier = pltpu.get_barrier_semaphore()
    for partner in (other, behind, ahead):
        pl.semaphore_signal(barrier, inc=1, device_id=(partner,), device_id_type=MESH)

    load_m = pltpu.make_async_copy(m_hbm, raw, load.at[0])
    load_t = pltpu.make_async_copy(t_hbm, text.at[0], load.at[1])
    load_x = pltpu.make_async_copy(x_hbm, near, load.at[2])
    small = [
        pltpu.make_async_copy(source, held, load.at[3 + i])
        for i, (source, held) in enumerate((
            (lag_hbm, lag), (slot_hbm, slot), (scales_hbm, scales),
            (multipliers_hbm, multipliers), (shifts_hbm, shifts),
        ))
    ]
    for copy in small:
        copy.start()
    load_m.start()
    load_t.start()
    load_x.start()
    small[0].wait()
    small[1].wait()
    code_mine[...] = lag[...] * rows + slot[...]
    regroup(code_mine, code_send)
    pl.semaphore_wait(barrier, 3)

    def remote(src, dst, send, recv, device):
        return pltpu.make_async_remote_copy(
            src_ref=src, dst_ref=dst, send_sem=send, recv_sem=recv,
            device_id=(device,), device_id_type=MESH,
        )

    def x_copy(i):
        at = pl.ds(i * chunk, chunk)
        return remote(x_hbm.at[at], far.at[at], x_ss.at[i], x_rs.at[i], behind)

    def g_copy(i):
        at = pl.ds(i * chunk, chunk)
        return remote(g_send.at[at], g_back.at[at], g_ss.at[i], g_rs.at[i], ahead)

    code_copy = remote(code_send, code_far, small_ss.at[0], small_rs.at[0], behind)
    loss_copy = remote(loss_far, loss_back, small_ss.at[1], small_rs.at[1], ahead)
    text_copy = remote(t_hbm, text.at[1], pair_ss.at[0], pair_rs.at[0], other)
    teacher_copy = remote(teacher.at[0], teacher.at[1], pair_ss.at[1], pair_rs.at[1], other)
    tg_copy = remote(tg_send, tg_back, pair_ss.at[2], pair_rs.at[2], other)

    code_copy.start()
    for i in range(steps):
        x_copy(i).start()
    text_copy.start()

    for copy in small[2:]:
        copy.wait()
    groups = scales.shape[0]
    exact = scales[...]
    high = exact.astype(BF16).astype(F32)
    middle = (exact - high).astype(BF16).astype(F32)
    low = exact - high - middle
    pieces = jnp.concatenate([high, middle, low], axis=0).astype(BF16)
    spread_rows = lax.rem(lax.broadcasted_iota(jnp.int32, (3 * groups, width), 0), groups)
    spread_cols = lax.broadcasted_iota(jnp.int32, (3 * groups, width), 1) // (width // groups)
    spread = jnp.where(spread_rows == spread_cols, F32(1.0), F32(0.0)).astype(BF16)
    load_m.wait()
    for start in range(0, rows, TILE):
        wide = dot(pieces[:, start:start + TILE], spread, 0, 0)
        teacher[0, start:start + TILE, :] = (raw[start:start + TILE, :].astype(F32) * wide).astype(BF16)
    teacher_copy.start()

    scale = F32(0.5 / math.sqrt(width))
    factors = (multipliers[0] * scale, multipliers[1] * scale)
    halves = (shifts[0] * 0.5, shifts[1] * 0.5)

    def students_grad(slope_t, slope_m, k):
        return dot(slope_t[...], text[k], 0, 0) * factors[0] + dot(slope_m[...], teacher[k], 0, 0) * factors[1]

    def near_step(k, n, carry):
        at = pl.ds(pl.multiple_of(n * TILE, TILE), TILE)
        per = TILE // lanes
        code = jnp.concatenate([code_mine[pl.ds(n * per + p, 1), :] for p in range(per)], axis=1)
        diagonal = lax.broadcasted_iota(jnp.int32, (1, TILE), 1) + n * TILE if k == 0 else None
        slope_t, slope_m = near_t.at[k, :, at], near_m
        loss = score(
            near[at, :], (text.at[k], teacher.at[k]), factors, halves, (code - k * rows, diagonal),
            (slope_t, slope_m),
        )
        grad = students_grad(slope_t, slope_m, k)
        for p in range(per):
            row = pl.ds(n * per + p, 1)
            part = loss[:, p * lanes:(p + 1) * lanes]
            loss_mine[row, :] = part if k == 0 else loss_mine[row, :] + part
        g_local[at, :] = grad if k == 0 else g_local[at, :] + grad
        return carry

    load_t.wait()
    load_x.wait()
    lax.fori_loop(0, wide_steps, lambda n, carry: near_step(0, n, carry), 0)
    code_copy.wait()
    text_copy.wait()
    teacher_copy.wait()

    def far_job(blocks, i):
        at = pl.ds(pl.multiple_of(i * chunk, chunk), chunk)
        row = pl.ds(i, 1)
        code = code_far[row, :]
        refs, hits, slopes = [], [], []
        for k in range(blocks):
            refs += [text.at[k], teacher.at[k]]
            hits += [code - (2 - k) * rows, None]
            slopes += [far_t.at[i, k], far_m.at[k]]
        loss_far[row, :] = score(far[at, :], refs, factors * blocks, halves * blocks, hits, slopes)
        grads = [
            sum(dot(slopes[2 * k + side][...], refs[2 * k + side][...], 0, 0) for k in range(blocks))
            for side in range(2)
        ]
        g_send[at, :] = (grads[0] * factors[0] + grads[1] * factors[1]).astype(BF16)

    def far_step(i, carry):
        x_copy(i).wait_recv()

        @pl.when(core == 0)
        def _():
            far_job(2, i)

        @pl.when(core == 1)
        def _():
            far_job(1, i)

        g_copy(i).start()

        @pl.when((core == 1) & (lax.rem(i, 2) == 0) & (i < 2 * wide_steps))
        def _():
            near_step(1, i // 2, 0)
        return carry

    def far_text_grad(k):
        slopes = jnp.concatenate([far_t[i, k] for i in range(steps)], axis=1)
        return dot(slopes, far[...], 1, 0)

    lax.fori_loop(0, steps, far_step, 0)
    loss_copy.start()

    @pl.when(core == 0)
    def _():
        tg_other[...] = far_text_grad(1)

    @pl.when(core == 1)
    def _():
        tg_other[...] = dot(near_t[1], near[...], 1, 0)

    tg_send[...] = tg_other[...].astype(BF16)
    tg_copy.start()
    tg_own[...] = dot(near_t[0], near[...], 1, 0)
    tg_own[...] += far_text_grad(0)

    for i in range(steps):
        at = pl.ds(i * chunk, chunk)
        g_copy(i).wait_recv()
        sg_out[at, :] = (g_local[at, :] + g_back[at, :].astype(F32)).astype(BF16)
        if i == steps // 2:
            tg_copy.wait()
            tg_out[...] = ((tg_own[...] + tg_back[...].astype(F32)) * factors[0]).astype(BF16)
    loss_copy.wait()
    regroup(loss_back, loss_wide)
    loss_out[...] = (loss_mine[...] + loss_wide[...]) * F32(1.0 / (3 * rows))
    for i in range(steps):
        x_copy(i).wait_send()
        g_copy(i).wait_send()


def write_out(*refs):
    count = len(refs) // 2
    done = refs[-1]
    copies = [pltpu.make_async_copy(refs[i], refs[count + i], done.at[i]) for i in range(count)]
    for copy in copies:
        copy.start()
    for copy in copies:
        copy.wait()


def body(
    pupil_vectors,
    caption_vectors,
    mentor_unscaled_entries,
    mentor_group_factors,
    partner_replica_lag,
    partner_entry_slot,
    logit_multipliers,
    logit_shifts,
):
    rows, width = pupil_vectors.shape
    chunk = CHUNK
    steps = rows // chunk
    lanes = 128
    hbm = pl.BlockSpec(memory_space=pl.ANY)
    vmem = pl.BlockSpec(memory_space=pltpu.VMEM)
    full_bf16 = pltpu.VMEM((rows, width), BF16)
    full_f32 = pltpu.VMEM((rows, width), F32)
    small_f32 = pltpu.VMEM((rows // lanes, lanes), F32)
    small_i32 = pltpu.VMEM((rows // lanes, lanes), jnp.int32)
    dma = pltpu.SemaphoreType.DMA
    results = pl.pallas_call(
        lambda *refs: kernel(chunk, *refs),
        name="distill",
        out_shape=(
            pltpu.VMEM((rows // lanes, lanes), F32),
            pltpu.VMEM((rows, width), BF16),
            pltpu.VMEM((rows, width), BF16),
        ),
        in_specs=[hbm] * 8,
        out_specs=(vmem, vmem, vmem),
        scratch_shapes=[
            pltpu.VMEM(mentor_group_factors.shape[::-1], F32),
            small_i32,
            small_i32,
            pltpu.SMEM(logit_multipliers.shape, F32),
            pltpu.SMEM(logit_shifts.shape, F32),
            full_bf16,
            full_bf16,
            pltpu.VMEM((2, rows, width), BF16),
            pltpu.VMEM((2, rows, width), BF16),
            full_bf16,
            pltpu.VMEM((2, rows, rows), BF16),
            pltpu.VMEM((rows, TILE), BF16),
            pltpu.VMEM((steps, 2, rows, chunk), BF16),
            pltpu.VMEM((2, rows, chunk), BF16),
            full_f32,
            full_f32,
            full_f32,
            full_bf16,
            full_bf16,
            full_bf16,
            full_bf16,
            small_i32,
            pltpu.VMEM((steps, chunk), jnp.int32),
            pltpu.VMEM((steps, chunk), jnp.int32),
            small_f32,
            pltpu.VMEM((steps, chunk), F32),
            pltpu.VMEM((steps, chunk), F32),
            small_f32,
            dma((steps,)), dma((steps,)), dma((steps,)), dma((steps,)),
            dma((3,)), dma((3,)), dma((2,)), dma((2,)),
            dma((8,)),
        ],
        compiler_params=pltpu.CompilerParams(
            collective_id=0, has_side_effects=True, vmem_limit_bytes=56 * 1024 * 1024
        ),
        cost_estimate=pl.CostEstimate(
            flops=30 * rows * rows * width, bytes_accessed=12 * rows * width, transcendentals=6 * rows * rows
        ),
    )(
        pupil_vectors,
        caption_vectors,
        mentor_unscaled_entries,
        mentor_group_factors.T,
        partner_replica_lag.reshape(rows // lanes, lanes),
        partner_entry_slot.reshape(rows // lanes, lanes),
        logit_multipliers,
        logit_shifts,
    )
    loss, student_grad, text_grad = pl.pallas_call(
        write_out,
        name="write_out",
        out_shape=(
            jax.ShapeDtypeStruct((rows // lanes, lanes), F32),
            jax.ShapeDtypeStruct((rows, width), BF16),
            jax.ShapeDtypeStruct((rows, width), BF16),
        ),
        in_specs=[vmem, vmem, vmem],
        out_specs=(hbm, hbm, hbm),
        scratch_shapes=[dma((3,))],
    )(*(pltpu.with_memory_space_constraint(result, pltpu.VMEM) for result in results))
    return loss.reshape(rows), student_grad, text_grad


def solution(mesh):
    placed = (
        P("batch", None),
        P("batch", None),
        P("batch", None),
        P("batch", None),
        P("batch"),
        P("batch"),
        P(),
        P(),
    )
    return jax.shard_map(
        body,
        mesh=mesh,
        in_specs=placed,
        out_specs=(P("batch"), P("batch", None), P("batch", None)),
        check_vma=False,
    )
```

```python
import math

import jax
import jax.numpy as jnp
from jax import lax
from jax.experimental import pallas as pl
from jax.experimental.pallas import tpu as pltpu
from jax.sharding import PartitionSpec as P

F32 = jnp.float32
BF16 = jnp.bfloat16
MESH = pl.DeviceIdType.MESH
LN2 = math.log(2.0)
TILE = 256
CHUNK = 96
GRID = (4, 8, 4)
X_RELAYED, X_FORWARD = 4, 3
G_RELAYED, G_FORWARD = 4, 7


def dot(a, b, ca, cb):
    return lax.dot_general(a, b, (((ca,), (cb,)), ((), ())), preferred_element_type=F32)


def score(students, refs, factors, shifts, hits, slopes):
    count = students.shape[0]
    width = refs[0].shape[0]
    total = jnp.zeros((1, count), F32)
    for ref, factor, shift, hit_row, slope in zip(refs, factors, shifts, hits, slopes):
        product = jnp.ones((8, count), F32)
        excess = jnp.zeros((8, count), F32)
        for start in range(0, width, TILE):
            half = dot(ref[start:start + TILE, :], students, 1, 1) * factor + shift
            sign = None
            if hit_row is not None:
                rows = lax.broadcasted_iota(jnp.int32, (TILE, count), 0)
                sign = jnp.where(rows == hit_row - start, F32(-1.0), F32(1.0))
                half = half * sign
            tanh = jnp.tanh(half)
            doubled = 1.0 + tanh
            if sign is not None:
                doubled = doubled * sign
            slope[start:start + TILE, :] = doubled.astype(BF16)
            folded = (1.0 + jnp.abs(tanh)).reshape(TILE // 8, 8, count)
            positive = jnp.maximum(half, 0.0).reshape(TILE // 8, 8, count)
            for part in range(TILE // 8):
                product = product * folded[part]
                excess = excess + positive[part]
        terms = 2.0 * excess - jnp.log(product)
        total = total + (jnp.sum(terms, axis=0, keepdims=True) + F32(width * LN2))
    return total


def regroup(source, target):
    long, short = source.shape[1], target.shape[1]
    for row in range(target.shape[0]):
        done = 0
        while done < short:
            line, column = divmod(row * short + done, long)
            count = min(short - done, long - column)
            target[row:row + 1, done:done + count] = source[line:line + 1, column:column + count]
            done += count


def kernel(
    chunk,
    x_hbm, t_hbm, m_hbm, scales_hbm, lag_hbm, slot_hbm, multipliers_hbm, shifts_hbm,
    loss_out, sg_out, tg_out,
    scales, lag, slot, multipliers, shifts,
    near, far, text, teacher, raw, near_t, near_m, far_t, far_m,
    tg_own, tg_other, g_local, g_send, g_back, tg_send, tg_back,
    code_mine, code_send, code_far, loss_mine, loss_far, loss_back, loss_wide,
    x_ss, x_rs, g_ss, g_rs, pair_ss, pair_rs, small_ss, small_rs, load,
    x_hold, g_hold, relay_ss, relay_rs, entered,
):
    rows, width = tg_own.shape
    lanes = lag.shape[1]
    steps = rows // chunk
    wide_steps = rows // TILE
    devices = lax.axis_size("batch")
    me = lax.axis_index("batch")
    core = lax.rem(me, 2)
    other = me + 1 - 2 * core
    behind = lax.rem(me + devices - 2, devices)
    ahead = lax.rem(me + 2, devices)

    nx, nz, ny = GRID
    x_at, z_at, y_at = me // (nz * ny * 2), lax.rem(me // (ny * 2), nz), lax.rem(me // 2, ny)

    def device(x, z, y):
        return ((lax.rem(x + nx, nx) * nz + z) * ny + y) * 2 + core

    is_source = (z_at == 0) & (y_at == 0)
    is_target = (z_at == nz - 1) & (y_at == ny - 1)
    is_x_relay = (z_at == 0) & (y_at == ny - 1)
    is_g_relay = (z_at == nz - 1) & (y_at == 0)
    source = device(x_at + 1, 0, 0)
    target = device(x_at, nz - 1, ny - 1)
    source_x_relay = device(x_at - 1, 0, ny - 1)
    target_x_relay = device(x_at, 0, ny - 1)
    target_g_relay = device(x_at + 1, nz - 1, 0)
    source_g_relay = device(x_at, nz - 1, 0)
    g_relay_source = device(x_at, 0, 0)
    g_relay_target = device(x_at - 1, nz - 1, ny - 1)

    barrier = pltpu.get_barrier_semaphore()

    def greet(partner):
        pl.semaphore_signal(barrier, inc=1, device_id=(partner,), device_id_type=MESH)

    for partner in (other, behind, ahead):
        greet(partner)

    @pl.when(is_source)
    def _():
        greet(source_g_relay)

    @pl.when(is_x_relay)
    def _():
        greet(source)
        greet(target)

    @pl.when(is_g_relay)
    def _():
        greet(g_relay_target)

    load_m = pltpu.make_async_copy(m_hbm, raw, load.at[0])
    load_t = pltpu.make_async_copy(t_hbm, text.at[0], load.at[1])
    load_x = pltpu.make_async_copy(x_hbm, near, load.at[2])
    small = [
        pltpu.make_async_copy(source, held, load.at[3 + i])
        for i, (source, held) in enumerate((
            (lag_hbm, lag), (slot_hbm, slot), (scales_hbm, scales),
            (multipliers_hbm, multipliers), (shifts_hbm, shifts),
        ))
    ]
    for copy in small:
        copy.start()
    load_m.start()
    load_t.start()
    load_x.start()
    small[0].wait()
    small[1].wait()
    code_mine[...] = lag[...] * rows + slot[...]
    regroup(code_mine, code_send)
    pl.semaphore_wait(barrier, 3 + jnp.where(is_target, 2, jnp.where(is_source | is_g_relay, 1, 0)))

    @pl.when(is_target)
    def _():
        pl.semaphore_signal(entered, inc=1, device_id=(target_x_relay,), device_id_type=MESH)

    def remote(src, dst, send, recv, device):
        return pltpu.make_async_remote_copy(
            src_ref=src, dst_ref=dst, send_sem=send, recv_sem=recv,
            device_id=(device,), device_id_type=MESH,
        )

    def x_copy(i):
        at = pl.ds(i * chunk, chunk)
        return remote(x_hbm.at[at], far.at[at], x_ss.at[i], x_rs.at[i], behind)

    def g_copy(i):
        at = pl.ds(i * chunk, chunk)
        return remote(g_send.at[at], g_back.at[at], g_ss.at[i], g_rs.at[i], ahead)

    step_x = pl.ds(X_RELAYED * chunk, chunk)
    step_g = pl.ds(G_RELAYED * chunk, chunk)
    x_to_relay = remote(
        x_hbm.at[step_x], x_hold, x_ss.at[X_RELAYED], relay_rs.at[0], source_x_relay
    )
    x_from_relay = remote(x_hold, far.at[step_x], relay_ss.at[0], x_rs.at[X_RELAYED], target)
    g_to_relay = remote(
        g_send.at[step_g], g_hold, g_ss.at[G_RELAYED], relay_rs.at[1], target_g_relay
    )
    g_from_relay = remote(g_hold, g_back.at[step_g], relay_ss.at[1], g_rs.at[G_RELAYED], g_relay_source)

    code_copy = remote(code_send, code_far, small_ss.at[0], small_rs.at[0], behind)
    loss_copy = remote(loss_far, loss_back, small_ss.at[1], small_rs.at[1], ahead)
    text_copy = remote(t_hbm, text.at[1], pair_ss.at[0], pair_rs.at[0], other)
    teacher_copy = remote(teacher.at[0], teacher.at[1], pair_ss.at[1], pair_rs.at[1], other)
    tg_copy = remote(tg_send, tg_back, pair_ss.at[2], pair_rs.at[2], other)

    code_copy.start()

    @pl.when(is_source)
    def _():
        x_to_relay.start()

    for i in range(steps):
        if i == X_RELAYED:
            pl.when(jnp.logical_not(is_source))(x_copy(i).start)
        else:
            x_copy(i).start()
    text_copy.start()

    for copy in small[2:]:
        copy.wait()
    groups = scales.shape[0]
    exact = scales[...]
    high = exact.astype(BF16).astype(F32)
    middle = (exact - high).astype(BF16).astype(F32)
    low = exact - high - middle
    pieces = jnp.concatenate([high, middle, low], axis=0).astype(BF16)
    spread_rows = lax.rem(lax.broadcasted_iota(jnp.int32, (3 * groups, width), 0), groups)
    spread_cols = lax.broadcasted_iota(jnp.int32, (3 * groups, width), 1) // (width // groups)
    spread = jnp.where(spread_rows == spread_cols, F32(1.0), F32(0.0)).astype(BF16)
    load_m.wait()
    for start in range(0, rows, TILE):
        wide = dot(pieces[:, start:start + TILE], spread, 0, 0)
        teacher[0, start:start + TILE, :] = (raw[start:start + TILE, :].astype(F32) * wide).astype(BF16)
    teacher_copy.start()

    scale = F32(0.5 / math.sqrt(width))
    factors = (multipliers[0] * scale, multipliers[1] * scale)
    halves = (shifts[0] * 0.5, shifts[1] * 0.5)

    def students_grad(slope_t, slope_m, k):
        return dot(slope_t[...], text[k], 0, 0) * factors[0] + dot(slope_m[...], teacher[k], 0, 0) * factors[1]

    def near_step(k, n, carry):
        at = pl.ds(pl.multiple_of(n * TILE, TILE), TILE)
        per = TILE // lanes
        code = jnp.concatenate([code_mine[pl.ds(n * per + p, 1), :] for p in range(per)], axis=1)
        diagonal = lax.broadcasted_iota(jnp.int32, (1, TILE), 1) + n * TILE if k == 0 else None
        slope_t, slope_m = near_t.at[k, :, at], near_m
        loss = score(
            near[at, :], (text.at[k], teacher.at[k]), factors, halves, (code - k * rows, diagonal),
            (slope_t, slope_m),
        )
        grad = students_grad(slope_t, slope_m, k)
        for p in range(per):
            row = pl.ds(n * per + p, 1)
            part = loss[:, p * lanes:(p + 1) * lanes]
            loss_mine[row, :] = part if k == 0 else loss_mine[row, :] + part
        g_local[at, :] = grad if k == 0 else g_local[at, :] + grad
        return carry

    load_t.wait()
    load_x.wait()
    lax.fori_loop(0, wide_steps, lambda n, carry: near_step(0, n, carry), 0)
    code_copy.wait()
    text_copy.wait()
    teacher_copy.wait()

    def far_job(blocks, i):
        at = pl.ds(pl.multiple_of(i * chunk, chunk), chunk)
        row = pl.ds(i, 1)
        code = code_far[row, :]
        refs, hits, slopes = [], [], []
        for k in range(blocks):
            refs += [text.at[k], teacher.at[k]]
            hits += [code - (2 - k) * rows, None]
            slopes += [far_t.at[i, k], far_m.at[k]]
        loss_far[row, :] = score(far[at, :], refs, factors * blocks, halves * blocks, hits, slopes)
        grads = [
            sum(dot(slopes[2 * k + side][...], refs[2 * k + side][...], 0, 0) for k in range(blocks))
            for side in range(2)
        ]
        g_send[at, :] = (grads[0] * factors[0] + grads[1] * factors[1]).astype(BF16)

    def far_step(i, carry):
        x_copy(i).wait_recv()

        @pl.when(core == 0)
        def _():
            far_job(2, i)

        @pl.when(core == 1)
        def _():
            far_job(1, i)

        @pl.when(is_target & (i == G_RELAYED))
        def _():
            g_to_relay.start()

        @pl.when(jnp.logical_not(is_target & (i == G_RELAYED)))
        def _():
            g_copy(i).start()

        @pl.when(is_x_relay & (i == X_FORWARD))
        def _():
            pl.semaphore_wait(entered, 1)
            x_to_relay.wait_recv()
            x_from_relay.start()

        @pl.when(is_g_relay & (i == G_FORWARD))
        def _():
            g_to_relay.wait_recv()
            g_from_relay.start()

        @pl.when((core == 1) & (lax.rem(i, 2) == 0) & (i < 2 * wide_steps))
        def _():
            near_step(1, i // 2, 0)
        return carry

    def far_text_grad(k):
        slopes = jnp.concatenate([far_t[i, k] for i in range(steps)], axis=1)
        return dot(slopes, far[...], 1, 0)

    lax.fori_loop(0, steps, far_step, 0)
    loss_copy.start()

    @pl.when(core == 0)
    def _():
        tg_other[...] = far_text_grad(1)

    @pl.when(core == 1)
    def _():
        tg_other[...] = dot(near_t[1], near[...], 1, 0)

    tg_send[...] = tg_other[...].astype(BF16)
    tg_copy.start()
    tg_own[...] = dot(near_t[0], near[...], 1, 0)
    tg_own[...] += far_text_grad(0)

    for i in range(steps):
        at = pl.ds(i * chunk, chunk)
        g_copy(i).wait_recv()
        sg_out[at, :] = (g_local[at, :] + g_back[at, :].astype(F32)).astype(BF16)
        if i == steps // 2:
            tg_copy.wait()
            tg_out[...] = ((tg_own[...] + tg_back[...].astype(F32)) * factors[0]).astype(BF16)
    loss_copy.wait()
    regroup(loss_back, loss_wide)
    loss_out[...] = (loss_mine[...] + loss_wide[...]) * F32(1.0 / (3 * rows))
    for i in range(steps):
        x_copy(i).wait_send()
        g_copy(i).wait_send()

    @pl.when(is_x_relay)
    def _():
        x_from_relay.wait_send()

    @pl.when(is_g_relay)
    def _():
        g_from_relay.wait_send()


def write_out(*refs):
    count = len(refs) // 2
    done = refs[-1]
    copies = [pltpu.make_async_copy(refs[i], refs[count + i], done.at[i]) for i in range(count)]
    for copy in copies:
        copy.start()
    for copy in copies:
        copy.wait()


def body(
    pupil_vectors,
    caption_vectors,
    mentor_unscaled_entries,
    mentor_group_factors,
    partner_replica_lag,
    partner_entry_slot,
    logit_multipliers,
    logit_shifts,
):
    rows, width = pupil_vectors.shape
    chunk = CHUNK
    steps = rows // chunk
    lanes = 128
    hbm = pl.BlockSpec(memory_space=pl.ANY)
    vmem = pl.BlockSpec(memory_space=pltpu.VMEM)
    full_bf16 = pltpu.VMEM((rows, width), BF16)
    full_f32 = pltpu.VMEM((rows, width), F32)
    small_f32 = pltpu.VMEM((rows // lanes, lanes), F32)
    small_i32 = pltpu.VMEM((rows // lanes, lanes), jnp.int32)
    dma = pltpu.SemaphoreType.DMA
    results = pl.pallas_call(
        lambda *refs: kernel(chunk, *refs),
        name="distill",
        out_shape=(
            pltpu.VMEM((rows // lanes, lanes), F32),
            pltpu.VMEM((rows, width), BF16),
            pltpu.VMEM((rows, width), BF16),
        ),
        in_specs=[hbm] * 8,
        out_specs=(vmem, vmem, vmem),
        scratch_shapes=[
            pltpu.VMEM(mentor_group_factors.shape[::-1], F32),
            small_i32,
            small_i32,
            pltpu.SMEM(logit_multipliers.shape, F32),
            pltpu.SMEM(logit_shifts.shape, F32),
            full_bf16,
            full_bf16,
            pltpu.VMEM((2, rows, width), BF16),
            pltpu.VMEM((2, rows, width), BF16),
            full_bf16,
            pltpu.VMEM((2, rows, rows), BF16),
            pltpu.VMEM((rows, TILE), BF16),
            pltpu.VMEM((steps, 2, rows, chunk), BF16),
            pltpu.VMEM((2, rows, chunk), BF16),
            full_f32,
            full_f32,
            full_f32,
            full_bf16,
            full_bf16,
            full_bf16,
            full_bf16,
            small_i32,
            pltpu.VMEM((steps, chunk), jnp.int32),
            pltpu.VMEM((steps, chunk), jnp.int32),
            small_f32,
            pltpu.VMEM((steps, chunk), F32),
            pltpu.VMEM((steps, chunk), F32),
            small_f32,
            dma((steps,)), dma((steps,)), dma((steps,)), dma((steps,)),
            dma((3,)), dma((3,)), dma((2,)), dma((2,)),
            dma((8,)),
            pltpu.VMEM((chunk, width), BF16),
            pltpu.VMEM((chunk, width), BF16),
            dma((2,)),
            dma((2,)),
            pltpu.SemaphoreType.REGULAR,
        ],
        compiler_params=pltpu.CompilerParams(
            collective_id=0, has_side_effects=True, vmem_limit_bytes=56 * 1024 * 1024
        ),
        cost_estimate=pl.CostEstimate(
            flops=30 * rows * rows * width, bytes_accessed=12 * rows * width, transcendentals=6 * rows * rows
        ),
    )(
        pupil_vectors,
        caption_vectors,
        mentor_unscaled_entries,
        mentor_group_factors.T,
        partner_replica_lag.reshape(rows // lanes, lanes),
        partner_entry_slot.reshape(rows // lanes, lanes),
        logit_multipliers,
        logit_shifts,
    )
    loss, student_grad, text_grad = pl.pallas_call(
        write_out,
        name="write_out",
        out_shape=(
            jax.ShapeDtypeStruct((rows // lanes, lanes), F32),
            jax.ShapeDtypeStruct((rows, width), BF16),
            jax.ShapeDtypeStruct((rows, width), BF16),
        ),
        in_specs=[vmem, vmem, vmem],
        out_specs=(hbm, hbm, hbm),
        scratch_shapes=[dma((3,))],
    )(*(pltpu.with_memory_space_constraint(result, pltpu.VMEM) for result in results))
    return loss.reshape(rows), student_grad, text_grad


def solution(mesh):
    placed = (
        P("batch", None),
        P("batch", None),
        P("batch", None),
        P("batch", None),
        P("batch"),
        P("batch"),
        P(),
        P(),
    )
    return jax.shard_map(
        body,
        mesh=mesh,
        in_specs=placed,
        out_specs=(P("batch"), P("batch", None), P("batch", None)),
        check_vma=False,
    )
```

```python
import math

import jax
import jax.numpy as jnp
from jax import lax
from jax.experimental import pallas as pl
from jax.experimental.pallas import tpu as pltpu
from jax.sharding import PartitionSpec as P

F32 = jnp.float32
BF16 = jnp.bfloat16
MESH = pl.DeviceIdType.MESH
LN2 = math.log(2.0)
TILE = 256
CHUNK = 96
GRID = (4, 8, 4)
X_RELAYED, X_FORWARD = 5, 3
G_RELAYED, G_FORWARD = 4, 6


def dot(a, b, ca, cb):
    return lax.dot_general(a, b, (((ca,), (cb,)), ((), ())), preferred_element_type=F32)


def score(students, refs, factors, shifts, hits, slopes):
    count = students.shape[0]
    width = refs[0].shape[0]
    total = jnp.zeros((1, count), F32)
    for ref, factor, shift, hit_row, slope in zip(refs, factors, shifts, hits, slopes):
        product = jnp.ones((8, count), F32)
        excess = jnp.zeros((8, count), F32)
        for start in range(0, width, TILE):
            half = dot(ref[start:start + TILE, :], students, 1, 1) * factor + shift
            sign = None
            if hit_row is not None:
                rows = lax.broadcasted_iota(jnp.int32, (TILE, count), 0)
                sign = jnp.where(rows == hit_row - start, F32(-1.0), F32(1.0))
                half = half * sign
            tanh = jnp.tanh(half)
            doubled = 1.0 + tanh
            if sign is not None:
                doubled = doubled * sign
            slope[start:start + TILE, :] = doubled.astype(BF16)
            folded = (1.0 + jnp.abs(tanh)).reshape(TILE // 8, 8, count)
            positive = jnp.maximum(half, 0.0).reshape(TILE // 8, 8, count)
            for part in range(TILE // 8):
                product = product * folded[part]
                excess = excess + positive[part]
        terms = 2.0 * excess - jnp.log(product)
        total = total + (jnp.sum(terms, axis=0, keepdims=True) + F32(width * LN2))
    return total


def regroup(source, target):
    long, short = source.shape[1], target.shape[1]
    for row in range(target.shape[0]):
        done = 0
        while done < short:
            line, column = divmod(row * short + done, long)
            count = min(short - done, long - column)
            target[row:row + 1, done:done + count] = source[line:line + 1, column:column + count]
            done += count


def kernel(
    chunk,
    x_hbm, t_hbm, m_hbm, scales_hbm, lag_hbm, slot_hbm, multipliers_hbm, shifts_hbm,
    loss_out, sg_out, tg_out,
    scales, lag, slot, multipliers, shifts,
    near, far, text, teacher, raw, near_t, near_m, far_t, far_m,
    tg_own, tg_other, g_local, g_send, g_back, tg_send, tg_back,
    code_mine, code_send, code_far, loss_mine, loss_far, loss_back, loss_wide,
    x_ss, x_rs, g_ss, g_rs, pair_ss, pair_rs, small_ss, small_rs, load,
    x_hold, g_hold, relay_ss, relay_rs, entered,
):
    rows, width = tg_own.shape
    lanes = lag.shape[1]
    steps = rows // chunk
    wide_steps = rows // TILE
    devices = lax.axis_size("batch")
    me = lax.axis_index("batch")
    core = lax.rem(me, 2)
    other = me + 1 - 2 * core
    behind = lax.rem(me + devices - 2, devices)
    ahead = lax.rem(me + 2, devices)

    nx, nz, ny = GRID
    x_at, z_at, y_at = me // (nz * ny * 2), lax.rem(me // (ny * 2), nz), lax.rem(me // 2, ny)

    def device(x, z, y):
        return ((lax.rem(x + nx, nx) * nz + z) * ny + y) * 2 + core

    is_source = (z_at == 0) & (y_at == 0)
    is_target = (z_at == nz - 1) & (y_at == ny - 1)
    is_x_relay = (z_at == 0) & (y_at == ny - 1)
    is_g_relay = (z_at == nz - 1) & (y_at == 0)
    source = device(x_at + 1, 0, 0)
    target = device(x_at, nz - 1, ny - 1)
    source_x_relay = device(x_at - 1, 0, ny - 1)
    target_x_relay = device(x_at, 0, ny - 1)
    target_g_relay = device(x_at + 1, nz - 1, 0)
    source_g_relay = device(x_at, nz - 1, 0)
    g_relay_source = device(x_at, 0, 0)
    g_relay_target = device(x_at - 1, nz - 1, ny - 1)

    barrier = pltpu.get_barrier_semaphore()

    def greet(partner):
        pl.semaphore_signal(barrier, inc=1, device_id=(partner,), device_id_type=MESH)

    for partner in (ahead, behind, other):
        greet(partner)

    @pl.when(is_source)
    def _():
        greet(source_g_relay)

    @pl.when(is_x_relay)
    def _():
        greet(source)
        greet(target)

    @pl.when(is_g_relay)
    def _():
        greet(g_relay_target)

    load_m = pltpu.make_async_copy(m_hbm, raw, load.at[0])
    load_t = pltpu.make_async_copy(t_hbm, text.at[0], load.at[1])
    load_x = pltpu.make_async_copy(x_hbm, near, load.at[2])
    small = [
        pltpu.make_async_copy(source, held, load.at[3 + i])
        for i, (source, held) in enumerate((
            (lag_hbm, lag), (slot_hbm, slot), (scales_hbm, scales),
            (multipliers_hbm, multipliers), (shifts_hbm, shifts),
        ))
    ]
    for copy in small:
        copy.start()
    load_m.start()
    load_t.start()
    load_x.start()
    small[0].wait()
    small[1].wait()
    code_mine[...] = lag[...] * rows + slot[...]
    regroup(code_mine, code_send)
    pl.semaphore_wait(barrier, 3 + jnp.where(is_target, 2, jnp.where(is_source | is_g_relay, 1, 0)))

    @pl.when(is_target)
    def _():
        pl.semaphore_signal(entered, inc=1, device_id=(target_x_relay,), device_id_type=MESH)

    def remote(src, dst, send, recv, device):
        return pltpu.make_async_remote_copy(
            src_ref=src, dst_ref=dst, send_sem=send, recv_sem=recv,
            device_id=(device,), device_id_type=MESH,
        )

    def x_copy(i):
        at = pl.ds(i * chunk, chunk)
        return remote(x_hbm.at[at], far.at[at], x_ss.at[i], x_rs.at[i], behind)

    def g_copy(i):
        at = pl.ds(i * chunk, chunk)
        return remote(g_send.at[at], g_back.at[at], g_ss.at[i], g_rs.at[i], ahead)

    step_x = pl.ds(X_RELAYED * chunk, chunk)
    step_g = pl.ds(G_RELAYED * chunk, chunk)
    x_to_relay = remote(
        x_hbm.at[step_x], x_hold, x_ss.at[X_RELAYED], relay_rs.at[0], source_x_relay
    )
    x_from_relay = remote(x_hold, far.at[step_x], relay_ss.at[0], x_rs.at[X_RELAYED], target)
    g_to_relay = remote(
        g_send.at[step_g], g_hold, g_ss.at[G_RELAYED], relay_rs.at[1], target_g_relay
    )
    g_from_relay = remote(g_hold, g_back.at[step_g], relay_ss.at[1], g_rs.at[G_RELAYED], g_relay_source)

    code_copy = remote(code_send, code_far, small_ss.at[0], small_rs.at[0], behind)
    loss_copy = remote(loss_far, loss_back, small_ss.at[1], small_rs.at[1], ahead)
    text_copy = remote(t_hbm, text.at[1], pair_ss.at[0], pair_rs.at[0], other)
    teacher_copy = remote(teacher.at[0], teacher.at[1], pair_ss.at[1], pair_rs.at[1], other)
    tg_copy = remote(tg_send, tg_back, pair_ss.at[2], pair_rs.at[2], other)

    code_copy.start()

    @pl.when(is_source)
    def _():
        x_to_relay.start()

    for i in range(steps):
        if i == X_RELAYED:
            pl.when(jnp.logical_not(is_source))(x_copy(i).start)
        else:
            x_copy(i).start()
    text_copy.start()

    for copy in small[2:]:
        copy.wait()
    groups = scales.shape[0]
    exact = scales[...]
    high = exact.astype(BF16).astype(F32)
    middle = (exact - high).astype(BF16).astype(F32)
    low = exact - high - middle
    pieces = jnp.concatenate([high, middle, low], axis=0).astype(BF16)
    spread_rows = lax.rem(lax.broadcasted_iota(jnp.int32, (3 * groups, width), 0), groups)
    spread_cols = lax.broadcasted_iota(jnp.int32, (3 * groups, width), 1) // (width // groups)
    spread = jnp.where(spread_rows == spread_cols, F32(1.0), F32(0.0)).astype(BF16)
    load_m.wait()
    for start in range(0, rows, TILE):
        wide = dot(pieces[:, start:start + TILE], spread, 0, 0)
        teacher[0, start:start + TILE, :] = (raw[start:start + TILE, :].astype(F32) * wide).astype(BF16)
    teacher_copy.start()

    scale = F32(0.5 / math.sqrt(width))
    factors = (multipliers[0] * scale, multipliers[1] * scale)
    halves = (shifts[0] * 0.5, shifts[1] * 0.5)

    def students_grad(slope_t, slope_m, k):
        return dot(slope_t[...], text[k], 0, 0) * factors[0] + dot(slope_m[...], teacher[k], 0, 0) * factors[1]

    def near_step(k, n, carry):
        at = pl.ds(pl.multiple_of(n * TILE, TILE), TILE)
        per = TILE // lanes
        code = jnp.concatenate([code_mine[pl.ds(n * per + p, 1), :] for p in range(per)], axis=1)
        diagonal = lax.broadcasted_iota(jnp.int32, (1, TILE), 1) + n * TILE if k == 0 else None
        slope_t, slope_m = near_t.at[k, :, at], near_m
        loss = score(
            near[at, :], (text.at[k], teacher.at[k]), factors, halves, (code - k * rows, diagonal),
            (slope_t, slope_m),
        )
        grad = students_grad(slope_t, slope_m, k)
        for p in range(per):
            row = pl.ds(n * per + p, 1)
            part = loss[:, p * lanes:(p + 1) * lanes]
            loss_mine[row, :] = part if k == 0 else loss_mine[row, :] + part
        g_local[at, :] = grad if k == 0 else g_local[at, :] + grad
        return carry

    load_t.wait()
    load_x.wait()
    lax.fori_loop(0, wide_steps, lambda n, carry: near_step(0, n, carry), 0)
    code_copy.wait()
    text_copy.wait()
    teacher_copy.wait()

    def far_job(blocks, i):
        at = pl.ds(pl.multiple_of(i * chunk, chunk), chunk)
        row = pl.ds(i, 1)
        code = code_far[row, :]
        refs, hits, slopes = [], [], []
        for k in range(blocks):
            refs += [text.at[k], teacher.at[k]]
            hits += [code - (2 - k) * rows, None]
            slopes += [far_t.at[i, k], far_m.at[k]]
        loss_far[row, :] = score(far[at, :], refs, factors * blocks, halves * blocks, hits, slopes)
        grads = [
            sum(dot(slopes[2 * k + side][...], refs[2 * k + side][...], 0, 0) for k in range(blocks))
            for side in range(2)
        ]
        g_send[at, :] = (grads[0] * factors[0] + grads[1] * factors[1]).astype(BF16)

    def far_step(i, carry):
        x_copy(i).wait_recv()

        @pl.when(core == 0)
        def _():
            far_job(2, i)

        @pl.when(core == 1)
        def _():
            far_job(1, i)

        @pl.when(is_target & (i == G_RELAYED))
        def _():
            g_to_relay.start()

        @pl.when(jnp.logical_not(is_target & (i == G_RELAYED)))
        def _():
            g_copy(i).start()

        @pl.when(is_x_relay & (i == X_FORWARD))
        def _():
            pl.semaphore_wait(entered, 1)
            x_to_relay.wait_recv()
            x_from_relay.start()

        @pl.when(is_g_relay & (i == G_FORWARD))
        def _():
            g_to_relay.wait_recv()
            g_from_relay.start()

        @pl.when((core == 1) & (lax.rem(i, 2) == 0) & (i < 2 * wide_steps))
        def _():
            near_step(1, i // 2, 0)
        return carry

    def far_text_grad(k):
        slopes = jnp.concatenate([far_t[i, k] for i in range(steps)], axis=1)
        return dot(slopes, far[...], 1, 0)

    lax.fori_loop(0, steps, far_step, 0)
    loss_copy.start()

    @pl.when(core == 0)
    def _():
        tg_other[...] = far_text_grad(1)

    @pl.when(core == 1)
    def _():
        tg_other[...] = dot(near_t[1], near[...], 1, 0)

    tg_send[...] = tg_other[...].astype(BF16)
    tg_copy.start()
    tg_own[...] = dot(near_t[0], near[...], 1, 0)
    tg_own[...] += far_text_grad(0)

    for i in range(steps):
        at = pl.ds(i * chunk, chunk)
        g_copy(i).wait_recv()
        sg_out[at, :] = (g_local[at, :] + g_back[at, :].astype(F32)).astype(BF16)
        if i == steps // 2:
            tg_copy.wait()
            tg_out[...] = ((tg_own[...] + tg_back[...].astype(F32)) * factors[0]).astype(BF16)
    loss_copy.wait()
    regroup(loss_back, loss_wide)
    loss_out[...] = (loss_mine[...] + loss_wide[...]) * F32(1.0 / (3 * rows))
    for i in range(steps):
        x_copy(i).wait_send()
        g_copy(i).wait_send()

    @pl.when(is_x_relay)
    def _():
        x_from_relay.wait_send()

    @pl.when(is_g_relay)
    def _():
        g_from_relay.wait_send()


def write_out(*refs):
    count = len(refs) // 2
    done = refs[-1]
    copies = [pltpu.make_async_copy(refs[i], refs[count + i], done.at[i]) for i in range(count)]
    for copy in copies:
        copy.start()
    for copy in copies:
        copy.wait()


def body(
    pupil_vectors,
    caption_vectors,
    mentor_unscaled_entries,
    mentor_group_factors,
    partner_replica_lag,
    partner_entry_slot,
    logit_multipliers,
    logit_shifts,
):
    rows, width = pupil_vectors.shape
    chunk = CHUNK
    steps = rows // chunk
    lanes = 128
    hbm = pl.BlockSpec(memory_space=pl.ANY)
    vmem = pl.BlockSpec(memory_space=pltpu.VMEM)
    full_bf16 = pltpu.VMEM((rows, width), BF16)
    full_f32 = pltpu.VMEM((rows, width), F32)
    small_f32 = pltpu.VMEM((rows // lanes, lanes), F32)
    small_i32 = pltpu.VMEM((rows // lanes, lanes), jnp.int32)
    dma = pltpu.SemaphoreType.DMA
    results = pl.pallas_call(
        lambda *refs: kernel(chunk, *refs),
        name="distill",
        out_shape=(
            pltpu.VMEM((rows // lanes, lanes), F32),
            pltpu.VMEM((rows, width), BF16),
            pltpu.VMEM((rows, width), BF16),
        ),
        in_specs=[hbm] * 8,
        out_specs=(vmem, vmem, vmem),
        scratch_shapes=[
            pltpu.VMEM(mentor_group_factors.shape[::-1], F32),
            small_i32,
            small_i32,
            pltpu.SMEM(logit_multipliers.shape, F32),
            pltpu.SMEM(logit_shifts.shape, F32),
            full_bf16,
            full_bf16,
            pltpu.VMEM((2, rows, width), BF16),
            pltpu.VMEM((2, rows, width), BF16),
            full_bf16,
            pltpu.VMEM((2, rows, rows), BF16),
            pltpu.VMEM((rows, TILE), BF16),
            pltpu.VMEM((steps, 2, rows, chunk), BF16),
            pltpu.VMEM((2, rows, chunk), BF16),
            full_f32,
            full_f32,
            full_f32,
            full_bf16,
            full_bf16,
            full_bf16,
            full_bf16,
            small_i32,
            pltpu.VMEM((steps, chunk), jnp.int32),
            pltpu.VMEM((steps, chunk), jnp.int32),
            small_f32,
            pltpu.VMEM((steps, chunk), F32),
            pltpu.VMEM((steps, chunk), F32),
            small_f32,
            dma((steps,)), dma((steps,)), dma((steps,)), dma((steps,)),
            dma((3,)), dma((3,)), dma((2,)), dma((2,)),
            dma((8,)),
            pltpu.VMEM((chunk, width), BF16),
            pltpu.VMEM((chunk, width), BF16),
            dma((2,)),
            dma((2,)),
            pltpu.SemaphoreType.REGULAR,
        ],
        compiler_params=pltpu.CompilerParams(
            collective_id=0, has_side_effects=True, vmem_limit_bytes=56 * 1024 * 1024
        ),
        cost_estimate=pl.CostEstimate(
            flops=30 * rows * rows * width, bytes_accessed=12 * rows * width, transcendentals=6 * rows * rows
        ),
    )(
        pupil_vectors,
        caption_vectors,
        mentor_unscaled_entries,
        mentor_group_factors.T,
        partner_replica_lag.reshape(rows // lanes, lanes),
        partner_entry_slot.reshape(rows // lanes, lanes),
        logit_multipliers,
        logit_shifts,
    )
    loss, student_grad, text_grad = pl.pallas_call(
        write_out,
        name="write_out",
        out_shape=(
            jax.ShapeDtypeStruct((rows // lanes, lanes), F32),
            jax.ShapeDtypeStruct((rows, width), BF16),
            jax.ShapeDtypeStruct((rows, width), BF16),
        ),
        in_specs=[vmem, vmem, vmem],
        out_specs=(hbm, hbm, hbm),
        scratch_shapes=[dma((3,))],
    )(*(pltpu.with_memory_space_constraint(result, pltpu.VMEM) for result in results))
    return loss.reshape(rows), student_grad, text_grad


def solution(mesh):
    placed = (
        P("batch", None),
        P("batch", None),
        P("batch", None),
        P("batch", None),
        P("batch"),
        P("batch"),
        P(),
        P(),
    )
    return jax.shard_map(
        body,
        mesh=mesh,
        in_specs=placed,
        out_specs=(P("batch"), P("batch", None), P("batch", None)),
        check_vma=False,
    )
```
